256 devices in a mesh: dp: 2 (over z_hi), pipe: 16 (over x, z_lo), tensor: 8 (over y, core).
Axes of the slice: x: 4, y: 4, z: 8 (z_hi: 2, z_lo: 4; z = z_hi * 4 + z_lo), core: 2. Of those that a mesh axis runs over, the one named last changes fastest.
Arguments:
- upstream: bfloat16 [16, 2, 1024, 6144], P('pipe', 'dp', 'tensor')
- inputs: bfloat16 [16, 2, 1024, 6144], P('pipe', 'dp', 'tensor')
- keys: bfloat16 [16, 2, 1024, 6144], P('pipe', 'dp', None, 'tensor')
- values: bfloat16 [16, 2, 1024, 6144], P('pipe', 'dp', None, 'tensor'), may hold values from -6 to 6
- gain: float32 [16, 6144], P('pipe'), may hold values from 0.5 to 1.5
Outputs:
- grad_inputs: bfloat16 [16, 2, 1024, 6144], P('pipe', 'dp', 'tensor')
- grad_keys: bfloat16 [16, 2, 1024, 6144], P('pipe', 'dp', None, 'tensor')
- grad_values: bfloat16 [16, 2, 1024, 6144], P('pipe', 'dp', None, 'tensor')
- grad_gain: float32 [16, 6144], P('pipe', 'tensor')
The draws below stay inside these ranges and needn't reach their ends.
All inputs are finite; a program needn't handle non-finite values.
Results may differ from the reference program's by a relative error of at most 0.02.
The reference program's roundings to bfloat16 on the way (of `incoming`, `normed_b`, `queries`, `weights_narrow`, `grad_scores` and `grad_queries`) count: a program that leaves them out, or rounds other values in their place, can miss the bound.
Values may be sent and summed in bfloat16 or wider, within the bound.
A program may use at most 192 MiB of HBM per device.

```python
import math
import jax
import jax.numpy as jnp
from jax import lax

HEADS = 48
HEAD_DIM = 128
D = 6144
SEQ = 1024
SECTIONS = 16
MICRO = 2


def base_rows(key):
    return jax.random.normal(jax.random.fold_in(key, 101), (SECTIONS, MICRO, SEQ, D), jnp.float32)


def draw_inputs(key, part):
    own_key = jax.random.fold_in(key, 1)
    samples = base_rows(key)
    logs = jax.random.uniform(own_key, (SECTIONS, MICRO, SEQ, 1), jnp.float32, math.log(0.3), math.log(3.0))
    return (samples * jnp.exp(logs)).astype(jnp.bfloat16)


def draw_keys(key, part):
    own_key = jax.random.fold_in(key, 2)
    drawn = 1.5 * jax.random.normal(jax.random.fold_in(own_key, 0), (SECTIONS, MICRO, SEQ, D), jnp.float32)
    return drawn.astype(jnp.bfloat16)


def draw_upstream(key, part):
    own_key = jax.random.fold_in(key, 3)
    samples = jax.random.normal(jax.random.fold_in(own_key, 0), (SECTIONS, MICRO, SEQ, D), jnp.float32)
    position_share = (jnp.arange(MICRO)[:, None] * SEQ + jnp.arange(SEQ)[None, :]).astype(jnp.float32) / (MICRO * SEQ - 1)
    rising = jnp.exp(math.log(3.0) * position_share)[None, :, :, None]
    return (samples * rising).astype(jnp.bfloat16)


def steps_of(key, dims, cuts, smallest, largest):
    def one(axis_at, shards_of):
        draws = jax.random.uniform(jax.random.fold_in(jax.random.fold_in(key, 6), axis_at), (shards_of,), jnp.float32, smallest / len(cuts), largest / len(cuts))
        return jnp.repeat(jnp.exp(draws), dims[axis_at] // shards_of).reshape((-1,) + (1,) * (len(dims) - axis_at - 1))

    factor_of = one(*cuts[0])
    for cut in cuts[1:]:
        factor_of = factor_of * one(*cut)
    return factor_of


def gaussian(rng, extent, scale, reach, split=(), held_as=jnp.bfloat16):
    loudness = steps_of(rng, extent, split, -0.22, 0.18) if split else 1.0
    values = jax.random.normal(rng, extent, jnp.float32) * scale * loudness
    return jnp.minimum(jnp.maximum(values, -reach), reach).astype(held_as)


def setup_inputs(seed: int = 0) -> dict:
    streams_of = jax.random.split(jax.random.key(seed), 6)
    upstream = draw_upstream(jax.random.fold_in(streams_of[5], 71), 0)
    inputs = draw_inputs(jax.random.fold_in(streams_of[5], 71), 0)
    keys = draw_keys(jax.random.fold_in(streams_of[5], 71), 0)
    values = gaussian(streams_of[3], (SECTIONS, MICRO, SEQ, D), 1.0, 6.0, ((0, 16), (1, 2), (3, 8)))
    gain = jnp.clip(1.0 + 0.1 * jax.random.normal(streams_of[4], (SECTIONS, D), jnp.float32), 0.5, 1.5)
    return {"upstream": upstream, "inputs": inputs, "keys": keys, "values": values, "gain": gain}


EPSILON = 1e-05

def narrow(value):
    return lax.optimization_barrier(value.astype(jnp.bfloat16))

def micro_backward(incoming, inputs, keys, values, gain):
    head_shape = (SEQ, HEADS, HEAD_DIM)
    inputs_wide = inputs.astype(jnp.float32)
    root_mean = jnp.sqrt(lax.optimization_barrier(jnp.mean(inputs_wide * inputs_wide, axis=-1, keepdims=True)) + EPSILON)
    normed = inputs_wide / root_mean
    normed_b = narrow(normed).astype(jnp.float32)
    queries = narrow(normed_b * gain).astype(jnp.float32)
    query_heads = queries.reshape(head_shape)
    key_heads = keys.astype(jnp.float32).reshape(head_shape)
    value_heads = values.astype(jnp.float32).reshape(head_shape)
    grad_out = incoming.astype(jnp.float32).reshape(head_shape)
    scaling = 1.0 / math.sqrt(HEAD_DIM)
    scores = jnp.einsum('qhd,khd->hqk', query_heads, key_heads) * scaling
    causal = jnp.arange(SEQ)[:, None] >= jnp.arange(SEQ)[None, :]
    scores = jnp.where(causal[None], scores, -jnp.inf)
    row_max = lax.optimization_barrier(jnp.max(scores, axis=-1, keepdims=True))
    log_total = row_max + jnp.log(lax.optimization_barrier(jnp.sum(jnp.exp(scores - row_max), axis=-1, keepdims=True)))
    softmax_weights = jnp.exp(scores - log_total)
    weights_narrow = narrow(softmax_weights).astype(jnp.float32)
    grad_weights = jnp.einsum('qhd,khd->hqk', grad_out, value_heads)
    row_delta = lax.optimization_barrier(jnp.sum(softmax_weights * grad_weights, axis=-1, keepdims=True))
    grad_scores = narrow(softmax_weights * (grad_weights - row_delta) * scaling).astype(jnp.float32)
    grad_values = jnp.einsum('hqk,qhd->khd', weights_narrow, grad_out).reshape(SEQ, D)
    grad_keys = jnp.einsum('hqk,qhd->khd', grad_scores, query_heads).reshape(SEQ, D)
    grad_queries = narrow(jnp.einsum('hqk,khd->qhd', grad_scores, key_heads).reshape(SEQ, D)).astype(jnp.float32)
    partial_gain = lax.optimization_barrier(jnp.sum(grad_queries * normed_b, axis=0))
    scaled = grad_queries * gain
    grad_inputs = incoming.astype(jnp.float32) + (scaled - normed * lax.optimization_barrier(jnp.mean(scaled * normed, axis=-1, keepdims=True))) / root_mean
    return (grad_inputs.astype(jnp.bfloat16), grad_keys.astype(jnp.bfloat16), grad_values.astype(jnp.bfloat16), partial_gain)

def section_backward(packed):
    incoming, inputs, keys, values, gain = packed

    def one_micro(pieces):
        return micro_backward(pieces[0], pieces[1], pieces[2], pieces[3], gain)
    results = lax.map(one_micro, (incoming, inputs, keys, values))
    return (results[0], results[1], results[2], lax.optimization_barrier(jnp.sum(results[3], axis=0)))

def reference(upstream, inputs, keys, values, gain):
    incoming = jnp.roll(upstream, -1, axis=0)
    grad_inputs, grad_keys, grad_values, grad_gain = lax.map(section_backward, (incoming, inputs, keys, values, gain))
    return (grad_inputs, grad_keys, grad_values, grad_gain)
```

```python
import functools
import math

import jax
import jax.numpy as jnp
from jax import lax
from jax.experimental import pallas as pl
from jax.experimental.pallas import tpu as pltpu
from jax.sharding import PartitionSpec as P

MESH = pl.DeviceIdType.MESH
HEAD_DIM = 128
EPSILON = 1e-05
ROWS = 256
F32 = jnp.float32
BF16 = jnp.bfloat16

NT = (((1,), (1,)), ((), ()))
NN = (((1,), (0,)), ((), ()))


def dot(a, b, dims):
    return lax.dot_general(a, b, dims, preferred_element_type=F32)


def fold(x, op):
    return op(x.reshape(x.shape[0] // 8, 8, x.shape[1]), axis=0)


def kernel(
    n_pipe, n_t, heads,
    up_hbm, x_hbm, k_hbm, v_hbm, gain_hbm,
    gi_hbm, dk_hbm, dv_hbm, gg_ref,
    x_s, gain_s, inv_s, nb, qn, up, go, dqs, dqr, k_s, v_s, q_s, kt_s,
    s_s, d_s, dk_acc, dv_acc, dk_b, dv_b, acc_s, out_b, pg, pgr,
    x_sem, gain_sem, k_sem, v_sem, nb_send, qn_recv, up_send, up_recv,
    go_send, go_recv, dq_send, dq_recv, pg_send, pg_recv, dk_sem, dv_sem, out_sem,
):
    d = lax.axis_index("dp")
    p = lax.axis_index("pipe")
    t = lax.axis_index("tensor")
    before = lax.rem(p + n_pipe - 1, n_pipe)
    after = lax.rem(p + 1, n_pipe)
    tokens = x_s.shape[0]
    length = n_t * tokens
    width = heads * HEAD_DIM
    features = n_t * width
    mine = pl.ds(pl.multiple_of(t * tokens, tokens), tokens)

    def peer(k):
        return lax.rem(t + k, n_t)

    barrier = pltpu.get_barrier_semaphore()

    def greet(k, carry):
        pl.semaphore_signal(barrier, inc=1, device_id=(d, p, peer(k)), device_id_type=MESH)
        return carry

    lax.fori_loop(1, n_t, greet, 0)
    pl.semaphore_signal(barrier, inc=1, device_id=(d, after, t), device_id_type=MESH)
    pl.semaphore_signal(barrier, inc=1, device_id=(1 - d, p, t), device_id_type=MESH)

    load_x = pltpu.make_async_copy(x_hbm, x_s, x_sem)
    load_x.start()
    load_gain = pltpu.make_async_copy(gain_hbm, gain_s, gain_sem)
    load_gain.start()

    def head_columns(h):
        return pl.ds(pl.multiple_of(h * HEAD_DIM, HEAD_DIM), HEAD_DIM)

    def load_k(h):
        return pltpu.make_async_copy(k_hbm.at[:, head_columns(h)], k_s.at[h], k_sem.at[h])

    def load_v(h):
        return pltpu.make_async_copy(v_hbm.at[:, head_columns(h)], v_s.at[h], v_sem.at[h])

    def start_loads(h, carry):
        load_k(h).start()
        load_v(h).start()
        return carry

    lax.fori_loop(0, heads, start_loads, 0)
    load_x.wait()

    def norm_rows(r, carry):
        rows = pl.ds(pl.multiple_of(r * 16, 16), 16)
        total = jnp.zeros((16, HEAD_DIM), F32)
        for c in range(n_t * heads):
            x = x_s[rows, c * HEAD_DIM : (c + 1) * HEAD_DIM].astype(F32)
            total = total + x * x
        mean = jnp.sum(total, axis=1, keepdims=True) * (1.0 / features)
        inv = jnp.broadcast_to(1.0 / jnp.sqrt(mean + EPSILON), (16, HEAD_DIM))
        inv_s[rows, :] = inv
        for c in range(n_t * heads):
            x = x_s[rows, c * HEAD_DIM : (c + 1) * HEAD_DIM].astype(F32)
            nb[c % heads, c // heads, rows, :] = (x * inv).astype(BF16)
        return carry

    lax.fori_loop(0, tokens // 16, norm_rows, 0)
    pg[...] = jnp.zeros_like(pg)

    pl.semaphore_wait(barrier, n_t + 1)

    def send_round(h, carry):
        def send_normed(k, carry):
            to = peer(k)
            pltpu.make_async_remote_copy(
                src_ref=nb.at[h, to], dst_ref=qn.at[h, mine, :],
                send_sem=nb_send.at[h], recv_sem=qn_recv.at[h],
                device_id=(d, p, to), device_id_type=MESH,
            ).start()
            return carry

        lax.fori_loop(1, n_t, send_normed, 0)
        pltpu.make_async_copy(nb.at[h, t], qn.at[h, mine, :], qn_recv.at[h]).start()

        def send_rows(j, carry):
            columns = pl.ds(pl.multiple_of((j * heads + h) * HEAD_DIM, HEAD_DIM), HEAD_DIM)
            pltpu.make_async_remote_copy(
                src_ref=up_hbm.at[:, columns], dst_ref=up.at[h, j],
                send_sem=up_send.at[h], recv_sem=up_recv.at[h],
                device_id=(d, before, t), device_id_type=MESH,
            ).start()
            return carry

        lax.fori_loop(0, n_t, send_rows, 0)
        return carry

    lax.fori_loop(0, heads, send_round, 0)
    load_gain.wait()

    def relay(h):
        pltpu.make_async_copy(up.at[h], up.at[h], up_recv.at[h]).wait()

        def send_grad(k, carry):
            to = peer(k)
            pltpu.make_async_remote_copy(
                src_ref=up.at[h, to], dst_ref=go.at[h, mine, :],
                send_sem=go_send.at[h], recv_sem=go_recv.at[h],
                device_id=(d, p, to), device_id_type=MESH,
            ).start()
            return carry

        lax.fori_loop(1, n_t, send_grad, 0)
        pltpu.make_async_copy(up.at[h, t], go.at[h, mine, :], go_recv.at[h]).start()

    to_base2 = math.log2(math.e) / math.sqrt(HEAD_DIM)
    scaling = 1.0 / math.sqrt(HEAD_DIM)
    blocks = length // ROWS
    below = lax.broadcasted_iota(jnp.int32, (ROWS, ROWS), 0) <= lax.broadcasted_iota(
        jnp.int32, (ROWS, ROWS), 1
    )

    def row_block(h, i):
        rows = pl.ds(i * ROWS, ROWS)
        q_i = q_s[rows, :]
        g_i = go[h, rows, :]
        top = None
        for c in range(i + 1):
            keys = pl.ds(c * ROWS, ROWS)
            s = dot(k_s[h, keys, :], q_i, NT)
            if c == i:
                s = jnp.where(below, s, -jnp.inf)
            s_s[keys, :] = s
            m = fold(s, jnp.max)
            top = m if top is None else jnp.maximum(top, m)
        top = jnp.max(top, axis=0, keepdims=True)
        total = jnp.zeros((8, ROWS), F32)
        weighted = jnp.zeros((8, ROWS), F32)
        for c in range(i + 1):
            keys = pl.ds(c * ROWS, ROWS)
            e = jnp.exp2((s_s[keys, :] - top) * to_base2)
            dp = dot(v_s[h, keys, :], g_i, NT)
            s_s[keys, :] = e
            d_s[keys, :] = dp
            total = total + fold(e, jnp.sum)
            weighted = weighted + fold(e * dp, jnp.sum)
        norm = 1.0 / jnp.sum(total, axis=0, keepdims=True)
        delta = jnp.sum(weighted, axis=0, keepdims=True) * norm
        norm_scaled = norm * scaling
        dq_t = jnp.zeros((HEAD_DIM, ROWS), F32)
        for c in range(i + 1):
            keys = pl.ds(c * ROWS, ROWS)
            e = s_s[keys, :]
            weights = (e * norm).astype(BF16)
            grad_s = ((e * norm_scaled) * (d_s[keys, :] - delta)).astype(BF16)
            dv = dot(weights, g_i, NN)
            dk = dot(grad_s, q_i, NN)
            if c == i:
                dv_acc[keys, :] = dv
                dk_acc[keys, :] = dk
            else:
                dv_acc[keys, :] += dv
                dk_acc[keys, :] += dk
            dq_t = dq_t + dot(kt_s[:, keys], grad_s, NN)
        dq = dq_t.T.astype(BF16)
        dqs[h, rows, :] = dq
        part = fold(dq.astype(F32) * qn[h, rows, :].astype(F32), jnp.sum)
        pg[pl.ds(h, 1), :] += jnp.sum(part, axis=0, keepdims=True)
        for b in range(ROWS // tokens):
            to = i * (ROWS // tokens) + b
            block = dqs.at[h, pl.ds(to * tokens, tokens), :]

            @pl.when(to != t)
            def _():
                pltpu.make_async_remote_copy(
                    src_ref=block, dst_ref=dqr.at[h, t],
                    send_sem=dq_send.at[h], recv_sem=dq_recv.at[h],
                    device_id=(d, p, to), device_id_type=MESH,
                ).start()

            @pl.when(to == t)
            def _():
                pltpu.make_async_copy(block, dqr.at[h, t], dq_recv.at[h]).start()

    def store_dk(h):
        return pltpu.make_async_copy(dk_b.at[h], dk_hbm.at[:, head_columns(h)], dk_sem.at[h])

    def store_dv(h):
        return pltpu.make_async_copy(dv_b.at[h], dv_hbm.at[:, head_columns(h)], dv_sem.at[h])

    def head(h, carry):
        @pl.when(h + 1 < heads)
        def _():
            relay(h + 1)

        load_k(h).wait()
        load_v(h).wait()
        kt_s[...] = k_s[h].T
        pltpu.make_async_copy(qn.at[h], qn.at[h], qn_recv.at[h]).wait()
        gain_row = gain_s[pl.ds(t * heads + h, 1), :]
        q_s[...] = (qn[h].astype(F32) * gain_row).astype(BF16)
        pltpu.make_async_copy(go.at[h], go.at[h], go_recv.at[h]).wait()
        for i in range(blocks):
            row_block(h, i)
        dk_b[h] = dk_acc[...].astype(BF16)
        dv_b[h] = dv_acc[...].astype(BF16)
        store_dk(h).start()
        store_dv(h).start()
        return carry

    relay(0)
    lax.fori_loop(0, heads, head, 0)

    share = pltpu.make_async_remote_copy(
        src_ref=pg, dst_ref=pgr, send_sem=pg_send, recv_sem=pg_recv,
        device_id=(1 - d, p, t), device_id_type=MESH,
    )
    share.start()

    acc_s[...] = jnp.zeros_like(acc_s)

    def arrived(h, carry):
        pltpu.make_async_copy(dqr.at[h], dqr.at[h], dq_recv.at[h]).wait()
        acc = acc_s[...]
        for j in range(n_t):
            columns = pl.ds(pl.multiple_of((j * heads + h) * HEAD_DIM, HEAD_DIM), HEAD_DIM)
            scaled = dqr[h, j].astype(F32) * gain_s[pl.ds(j * heads + h, 1), :]
            acc = acc + scaled * x_s[:, columns].astype(F32)
        acc_s[...] = acc
        return carry

    lax.fori_loop(0, heads, arrived, 0)
    inv = inv_s[...]
    shift = jnp.sum(acc_s[...], axis=1, keepdims=True) * (1.0 / features) * (inv * inv * inv)
    acc_s[...] = shift

    def store_out(j):
        columns = pl.ds(pl.multiple_of(j * width, HEAD_DIM), width)
        return pltpu.make_async_copy(out_b.at[:, columns], gi_hbm.at[:, columns], out_sem.at[j])

    def finish(j, carry):
        inv = inv_s[...]
        shift = acc_s[...]
        for h in range(heads):
            columns = pl.ds(pl.multiple_of((j * heads + h) * HEAD_DIM, HEAD_DIM), HEAD_DIM)
            scaled = dqr[h, j].astype(F32) * gain_s[pl.ds(j * heads + h, 1), :]
            x = x_s[:, columns].astype(F32)
            out = up[h, j].astype(F32) + (scaled * inv - x * shift)
            out_b[:, columns] = out.astype(BF16)
        store_out(j).start()
        return carry

    lax.fori_loop(0, n_t, finish, 0)

    share.wait()
    summed = pg[...] + pgr[...]
    for h in range(heads):
        gg_ref[:, h * HEAD_DIM : (h + 1) * HEAD_DIM] = summed[h : h + 1, :]

    def drain(h, carry):
        many = pl.ds(0, n_t - 1)
        pltpu.make_async_copy(nb.at[h, many], nb.at[h, many], nb_send.at[h]).wait()
        pltpu.make_async_copy(up.at[h], up.at[h], up_send.at[h]).wait()
        pltpu.make_async_copy(nb.at[h, many], nb.at[h, many], go_send.at[h]).wait()
        pltpu.make_async_copy(nb.at[h, many], nb.at[h, many], dq_send.at[h]).wait()
        store_dk(h).wait()
        store_dv(h).wait()
        return carry

    lax.fori_loop(0, heads, drain, 0)

    def drain_out(j, carry):
        store_out(j).wait()
        return carry

    lax.fori_loop(0, n_t, drain_out, 0)


def body(n_pipe, n_t, upstream, inputs, keys, values, gain):
    tokens, features = inputs.shape[2:]
    length, width = keys.shape[2:]
    heads = width // HEAD_DIM
    dma = pltpu.SemaphoreType.DMA
    rounds = pltpu.VMEM((heads, n_t, tokens, HEAD_DIM), BF16)
    by_head = pltpu.VMEM((heads, length, HEAD_DIM), BF16)
    anywhere = pl.BlockSpec(memory_space=pl.ANY)
    grad_inputs, grad_keys, grad_values, grad_gain = pl.pallas_call(
        functools.partial(kernel, n_pipe, n_t, heads),
        out_shape=(
            jax.ShapeDtypeStruct((tokens, features), BF16),
            jax.ShapeDtypeStruct((length, width), BF16),
            jax.ShapeDtypeStruct((length, width), BF16),
            jax.ShapeDtypeStruct((1, width), F32),
        ),
        in_specs=[anywhere] * 5,
        out_specs=(anywhere, anywhere, anywhere, pl.BlockSpec(memory_space=pltpu.VMEM)),
        scratch_shapes=[
            pltpu.VMEM((tokens, features), BF16),
            pltpu.VMEM((n_t * heads, HEAD_DIM), F32),
            pltpu.VMEM((tokens, HEAD_DIM), F32),
            rounds, by_head, rounds, by_head, by_head, rounds,
            by_head, by_head,
            pltpu.VMEM((length, HEAD_DIM), BF16),
            pltpu.VMEM((HEAD_DIM, length), BF16),
            pltpu.VMEM((length, ROWS), F32),
            pltpu.VMEM((length, ROWS), F32),
            pltpu.VMEM((length, HEAD_DIM), F32),
            pltpu.VMEM((length, HEAD_DIM), F32),
            by_head, by_head,
            pltpu.VMEM((tokens, HEAD_DIM), F32),
            pltpu.VMEM((tokens, features), BF16),
            pltpu.VMEM((8, HEAD_DIM), F32),
            pltpu.VMEM((8, HEAD_DIM), F32),
            dma, dma,
            dma((heads,)), dma((heads,)),
            dma((heads,)), dma((heads,)), dma((heads,)), dma((heads,)),
            dma((heads,)), dma((heads,)), dma((heads,)), dma((heads,)),
            dma, dma,
            dma((heads,)), dma((heads,)), dma((n_t,)),
        ],
        compiler_params=pltpu.CompilerParams(
            collective_id=0, has_side_effects=True, vmem_limit_bytes=48 * 2**20
        ),
    )(
        upstream.reshape(tokens, features),
        inputs.reshape(tokens, features),
        keys.reshape(length, width),
        values.reshape(length, width),
        gain.reshape(n_t * heads, HEAD_DIM),
    )
    return (
        grad_inputs.reshape(inputs.shape),
        grad_keys.reshape(keys.shape),
        grad_values.reshape(values.shape),
        grad_gain,
    )


def solution(mesh):
    in_specs = (
        P("pipe", "dp", "tensor", None),
        P("pipe", "dp", "tensor", None),
        P("pipe", "dp", None, "tensor"),
        P("pipe", "dp", None, "tensor"),
        P("pipe", None),
    )
    out_specs = (
        P("pipe", "dp", "tensor", None),
        P("pipe", "dp", None, "tensor"),
        P("pipe", "dp", None, "tensor"),
        P("pipe", "tensor"),
    )
    step = functools.partial(body, mesh.shape["pipe"], mesh.shape["tensor"])
    return jax.shard_map(step, mesh=mesh, in_specs=in_specs, out_specs=out_specs, check_vma=False)
```

```python
import functools
import math

import jax
import jax.numpy as jnp
from jax import lax
from jax.experimental import pallas as pl
from jax.experimental.pallas import tpu as pltpu
from jax.sharding import PartitionSpec as P

MESH = pl.DeviceIdType.MESH
HEAD_DIM = 128
EPSILON = 1e-05
ROWS = 256
FIRST = 4
AHEAD = 3
PIECES = 4
F32 = jnp.float32
BF16 = jnp.bfloat16

NT = (((1,), (1,)), ((), ()))
NN = (((1,), (0,)), ((), ()))


def dot(a, b, dims):
    return lax.dot_general(a, b, dims, preferred_element_type=F32)


def fold(x, op):
    return op(x.reshape(x.shape[0] // 8, 8, x.shape[1]), axis=0)


def kernel(
    n_pipe, n_t, heads,
    up_hbm, x_hbm, k_hbm, v_hbm, gain_hbm,
    part_ref, x_s, shift_ref, dk_ref, dv_ref, gg_ref,
    gain_s, inv_s, nb, qn, up, go, dqs, dqr, k_s, v_s, q_s, kt_s,
    s_s, d_s, dk_acc, dv_acc, acc_s, pg, pgr,
    x_sem, gain_sem, k_sem, v_sem, nb_send, qn_recv, up_send, up_recv,
    go_send, go_recv, dq_send, dq_recv, pg_send, pg_recv, pair_sem,
):
    d = lax.axis_index("dp")
    p = lax.axis_index("pipe")
    t = lax.axis_index("tensor")
    before = lax.rem(p + n_pipe - 1, n_pipe)
    after = lax.rem(p + 1, n_pipe)
    tokens = x_s.shape[0]
    length = n_t * tokens
    width = heads * HEAD_DIM
    features = n_t * width
    mine = pl.ds(pl.multiple_of(t * tokens, tokens), tokens)

    def peer(k):
        return lax.rem(t + k, n_t)

    barrier = pltpu.get_barrier_semaphore()

    def greet(k, carry):
        pl.semaphore_signal(barrier, inc=1, device_id=(d, p, peer(k)), device_id_type=MESH)
        return carry

    lax.fori_loop(1, n_t, greet, 0)
    second = lax.rem(t, 2)
    own_second = t - second + 1
    pl.semaphore_signal(barrier, inc=1, device_id=(d, after, own_second), device_id_type=MESH)
    pl.semaphore_signal(barrier, inc=1, device_id=(1 - d, p, own_second), device_id_type=MESH)

    load_x = pltpu.make_async_copy(x_hbm, x_s, x_sem)
    load_x.start()
    load_gain = pltpu.make_async_copy(gain_hbm, gain_s, gain_sem)
    load_gain.start()

    def head_columns(h):
        return pl.ds(pl.multiple_of(h * HEAD_DIM, HEAD_DIM), HEAD_DIM)

    def load_k(h):
        return pltpu.make_async_copy(k_hbm.at[:, head_columns(h)], k_s.at[h], k_sem.at[h])

    def load_v(h):
        return pltpu.make_async_copy(v_hbm.at[:, head_columns(h)], v_s.at[h], v_sem.at[h])

    def start_loads(h, carry):
        load_k(h).start()
        load_v(h).start()
        return carry

    lax.fori_loop(0, heads, start_loads, 0)
    load_x.wait()

    def norm_rows(r, carry):
        rows = pl.ds(pl.multiple_of(r * 16, 16), 16)
        total = jnp.zeros((16, HEAD_DIM), F32)
        for c in range(n_t * heads):
            x = x_s[rows, c * HEAD_DIM : (c + 1) * HEAD_DIM].astype(F32)
            total = total + x * x
        mean = jnp.sum(total, axis=1, keepdims=True) * (1.0 / features)
        inv = jnp.broadcast_to(1.0 / jnp.sqrt(mean + EPSILON), (16, HEAD_DIM))
        inv_s[rows, :] = inv
        for c in range(n_t * heads):
            x = x_s[rows, c * HEAD_DIM : (c + 1) * HEAD_DIM].astype(F32)
            nb[c % heads, c // heads, rows, :] = (x * inv).astype(BF16)
        return carry

    lax.fori_loop(0, tokens // 16, norm_rows, 0)
    pg[...] = jnp.zeros_like(pg)

    def send_normed_round(h):
        def send_normed(k, carry):
            to = peer(k)
            pltpu.make_async_remote_copy(
                src_ref=nb.at[h, to], dst_ref=qn.at[h, mine, :],
                send_sem=nb_send.at[h], recv_sem=qn_recv.at[h],
                device_id=(d, p, to), device_id_type=MESH,
            ).start()
            return carry

        lax.fori_loop(1, n_t, send_normed, 0)
        pltpu.make_async_copy(nb.at[h, t], qn.at[h, mine, :], qn_recv.at[h]).start()

    def send_rows_round(h, carry):
        def send_rows(j, carry):
            columns = pl.ds(pl.multiple_of((j * heads + h) * HEAD_DIM, HEAD_DIM), HEAD_DIM)
            pltpu.make_async_remote_copy(
                src_ref=up_hbm.at[:, columns], dst_ref=up.at[h, j],
                send_sem=up_send.at[h], recv_sem=up_recv.at[h],
                device_id=(d, before, t), device_id_type=MESH,
            ).start()
            return carry

        lax.fori_loop(0, n_t, send_rows, 0)
        return carry

    @pl.when(second == 0)
    def _():
        pl.semaphore_wait(barrier, n_t - 1)
        for h in range(min(FIRST, heads)):
            send_normed_round(h)
        pl.semaphore_wait(pair_sem, 1)
        lax.fori_loop(0, heads, send_rows_round, 0)

    @pl.when(second == 1)
    def _():
        pl.semaphore_wait(barrier, n_t + 3)
        pl.semaphore_signal(pair_sem, inc=1, device_id=(d, p, t - 1), device_id_type=MESH)
        send_rows_round(0, 0)
        for h in range(min(FIRST, heads)):
            send_normed_round(h)
        lax.fori_loop(1, heads, send_rows_round, 0)

    load_gain.wait()

    def relay(h):
        pltpu.make_async_copy(up.at[h], up.at[h], up_recv.at[h]).wait()

        def send_grad(k, carry):
            to = peer(k)
            pltpu.make_async_remote_copy(
                src_ref=up.at[h, to], dst_ref=go.at[h, mine, :],
                send_sem=go_send.at[h], recv_sem=go_recv.at[h],
                device_id=(d, p, to), device_id_type=MESH,
            ).start()
            return carry

        lax.fori_loop(1, n_t, send_grad, 0)
        pltpu.make_async_copy(up.at[h, t], go.at[h, mine, :], go_recv.at[h]).start()

        @pl.when(h + FIRST < heads)
        def _():
            send_normed_round(h + FIRST)

    to_base2 = math.log2(math.e) / math.sqrt(HEAD_DIM)
    scaling = 1.0 / math.sqrt(HEAD_DIM)
    blocks = length // ROWS
    below = lax.broadcasted_iota(jnp.int32, (ROWS, ROWS), 0) <= lax.broadcasted_iota(
        jnp.int32, (ROWS, ROWS), 1
    )

    def row_block(h, i):
        rows = pl.ds(i * ROWS, ROWS)
        q_i = q_s[rows, :]
        g_i = go[h, rows, :]
        top = None
        for c in range(i + 1):
            keys = pl.ds(c * ROWS, ROWS)
            s = dot(k_s[h, keys, :], q_i, NT)
            if c == i:
                s = jnp.where(below, s, -jnp.inf)
            s_s[keys, :] = s
            m = fold(s, jnp.max)
            top = m if top is None else jnp.maximum(top, m)
        top = jnp.max(top, axis=0, keepdims=True)
        total = jnp.zeros((8, ROWS), F32)
        weighted = jnp.zeros((8, ROWS), F32)
        for c in range(i + 1):
            keys = pl.ds(c * ROWS, ROWS)
            e = jnp.exp2((s_s[keys, :] - top) * to_base2)
            dp = dot(v_s[h, keys, :], g_i, NT)
            s_s[keys, :] = e
            d_s[keys, :] = dp
            total = total + fold(e, jnp.sum)
            weighted = weighted + fold(e * dp, jnp.sum)
        norm = 1.0 / jnp.sum(total, axis=0, keepdims=True)
        delta = jnp.sum(weighted, axis=0, keepdims=True) * norm
        norm_scaled = norm * scaling
        dq_t = jnp.zeros((HEAD_DIM, ROWS), F32)
        for c in range(i + 1):
            keys = pl.ds(c * ROWS, ROWS)
            e = s_s[keys, :]
            weights = (e * norm).astype(BF16)
            grad_s = ((e * norm_scaled) * (d_s[keys, :] - delta)).astype(BF16)
            dv = dot(weights, g_i, NN)
            dk = dot(grad_s, q_i, NN)
            if c == i:
                dv_acc[keys, :] = dv
                dk_acc[keys, :] = dk
            else:
                dv_acc[keys, :] += dv
                dk_acc[keys, :] += dk
            dq_t = dq_t + dot(kt_s[:, keys], grad_s, NN)
        dq = dq_t.T.astype(BF16)
        dqs[h, rows, :] = dq
        part = fold(dq.astype(F32) * qn[h, rows, :].astype(F32), jnp.sum)
        pg[pl.ds(h, 1), :] += jnp.sum(part, axis=0, keepdims=True)

    def send_dq_round(h):
        def send_dq(k, carry):
            to = peer(k)
            pltpu.make_async_remote_copy(
                src_ref=dqs.at[h, pl.ds(pl.multiple_of(to * tokens, tokens), tokens), :],
                dst_ref=dqr.at[h, t],
                send_sem=dq_send.at[h], recv_sem=dq_recv.at[h],
                device_id=(d, p, to), device_id_type=MESH,
            ).start()
            return carry

        lax.fori_loop(1, n_t, send_dq, 0)
        pltpu.make_async_copy(dqs.at[h, mine, :], dqr.at[h, t], dq_recv.at[h]).start()

    def head(h, carry):
        load_k(h).wait()
        load_v(h).wait()
        kt_s[...] = k_s[h].T
        pltpu.make_async_copy(qn.at[h], qn.at[h], qn_recv.at[h]).wait()
        gain_row = gain_s[pl.ds(t * heads + h, 1), :]
        q_s[...] = (qn[h].astype(F32) * gain_row).astype(BF16)
        pltpu.make_async_copy(go.at[h], go.at[h], go_recv.at[h]).wait()
        for i in range(blocks):
            row_block(h, i)

        send_dq_round(h)

        @pl.when(h + AHEAD < heads)
        def _():
            relay(h + AHEAD)

        dk_ref[:, head_columns(h)] = dk_acc[...].astype(BF16)
        dv_ref[:, head_columns(h)] = dv_acc[...].astype(BF16)
        return carry

    for h in range(min(AHEAD, heads)):
        relay(h)
    lax.fori_loop(0, heads, head, 0)

    share = pltpu.make_async_remote_copy(
        src_ref=pg, dst_ref=pgr, send_sem=pg_send, recv_sem=pg_recv,
        device_id=(1 - d, p, t), device_id_type=MESH,
    )
    share.start()

    acc_s[...] = jnp.zeros_like(acc_s)

    def arrived(h, carry):
        pltpu.make_async_copy(dqr.at[h], dqr.at[h], dq_recv.at[h]).wait()
        acc = acc_s[...]
        inv = inv_s[...]
        for j in range(n_t):
            columns = pl.ds(pl.multiple_of((j * heads + h) * HEAD_DIM, HEAD_DIM), HEAD_DIM)
            scaled = dqr[h, j].astype(F32) * gain_s[pl.ds(j * heads + h, 1), :]
            acc = acc + scaled * x_s[:, columns].astype(F32)
            part_ref[:, columns] = up[h, j].astype(F32) + scaled * inv
        acc_s[...] = acc
        return carry

    lax.fori_loop(0, heads, arrived, 0)
    inv = inv_s[...]
    shift_ref[...] = jnp.sum(acc_s[...], axis=1, keepdims=True) * (1.0 / features) * (inv * inv * inv)

    share.wait()
    summed = pg[...] + pgr[...]
    for h in range(heads):
        gg_ref[:, h * HEAD_DIM : (h + 1) * HEAD_DIM] = summed[h : h + 1, :]

    def drain(h, carry):
        many = pl.ds(0, n_t - 1)
        pltpu.make_async_copy(nb.at[h, many], nb.at[h, many], nb_send.at[h]).wait()
        pltpu.make_async_copy(up.at[h], up.at[h], up_send.at[h]).wait()
        pltpu.make_async_copy(nb.at[h, many], nb.at[h, many], go_send.at[h]).wait()
        pltpu.make_async_copy(nb.at[h, many], nb.at[h, many], dq_send.at[h]).wait()
        return carry

    lax.fori_loop(0, heads, drain, 0)


def finish_kernel(
    part_ref, x_ref, shift_ref, dk_ref, dv_ref, gg_ref,
    gi_out, dk_out, dv_out, gg_out, gi_b, sem, gi_sem,
):
    stores = [
        pltpu.make_async_copy(dk_ref, dk_out, sem.at[0]),
        pltpu.make_async_copy(dv_ref, dv_out, sem.at[1]),
        pltpu.make_async_copy(gg_ref, gg_out, sem.at[2]),
    ]
    for store in stores:
        store.start()
    width = gi_b.shape[1] // PIECES
    for j in range(PIECES):
        for c in range(j * width, (j + 1) * width, HEAD_DIM):
            columns = slice(c, c + HEAD_DIM)
            out = part_ref[:, columns] - x_ref[:, columns].astype(F32) * shift_ref[...]
            gi_b[:, columns] = out.astype(BF16)
        columns = slice(j * width, (j + 1) * width)
        store = pltpu.make_async_copy(gi_b.at[:, columns], gi_out.at[:, columns], gi_sem.at[j])
        store.start()
        stores.append(store)
    for store in stores:
        store.wait()


def body(n_pipe, n_t, upstream, inputs, keys, values, gain):
    tokens, features = inputs.shape[2:]
    length, width = keys.shape[2:]
    heads = width // HEAD_DIM
    dma = pltpu.SemaphoreType.DMA
    rounds = pltpu.VMEM((heads, n_t, tokens, HEAD_DIM), BF16)
    by_head = pltpu.VMEM((heads, length, HEAD_DIM), BF16)
    anywhere = pl.BlockSpec(memory_space=pl.ANY)
    in_vmem = pl.BlockSpec(memory_space=pltpu.VMEM)
    results = pl.pallas_call(
        functools.partial(kernel, n_pipe, n_t, heads),
        out_shape=(
            pltpu.VMEM((tokens, features), F32),
            pltpu.VMEM((tokens, features), BF16),
            pltpu.VMEM((tokens, HEAD_DIM), F32),
            pltpu.VMEM((length, width), BF16),
            pltpu.VMEM((length, width), BF16),
            pltpu.VMEM((1, width), F32),
        ),
        in_specs=[anywhere] * 5,
        out_specs=(in_vmem,) * 6,
        scratch_shapes=[
            pltpu.VMEM((n_t * heads, HEAD_DIM), F32),
            pltpu.VMEM((tokens, HEAD_DIM), F32),
            rounds, by_head, rounds, by_head, by_head, rounds,
            by_head, by_head,
            pltpu.VMEM((length, HEAD_DIM), BF16),
            pltpu.VMEM((HEAD_DIM, length), BF16),
            pltpu.VMEM((length, ROWS), F32),
            pltpu.VMEM((length, ROWS), F32),
            pltpu.VMEM((length, HEAD_DIM), F32),
            pltpu.VMEM((length, HEAD_DIM), F32),
            pltpu.VMEM((tokens, HEAD_DIM), F32),
            pltpu.VMEM((8, HEAD_DIM), F32),
            pltpu.VMEM((8, HEAD_DIM), F32),
            dma, dma,
            dma((heads,)), dma((heads,)),
            dma((heads,)), dma((heads,)), dma((heads,)), dma((heads,)),
            dma((heads,)), dma((heads,)), dma((heads,)), dma((heads,)),
            dma, dma,
            pltpu.SemaphoreType.REGULAR,
        ],
        compiler_params=pltpu.CompilerParams(
            collective_id=0, has_side_effects=True, vmem_limit_bytes=48 * 2**20
        ),
    )(
        upstream.reshape(tokens, features),
        inputs.reshape(tokens, features),
        keys.reshape(length, width),
        values.reshape(length, width),
        gain.reshape(n_t * heads, HEAD_DIM),
    )
    results = [pltpu.with_memory_space_constraint(r, pltpu.VMEM) for r in results]
    grad_inputs, grad_keys, grad_values, grad_gain = pl.pallas_call(
        finish_kernel,
        out_shape=(
            jax.ShapeDtypeStruct((tokens, features), BF16),
            jax.ShapeDtypeStruct((length, width), BF16),
            jax.ShapeDtypeStruct((length, width), BF16),
            jax.ShapeDtypeStruct((1, width), F32),
        ),
        in_specs=[in_vmem] * 6,
        out_specs=(anywhere,) * 4,
        scratch_shapes=[pltpu.VMEM((tokens, features), BF16), dma((3,)), dma((PIECES,))],
        compiler_params=pltpu.CompilerParams(vmem_limit_bytes=8 * 2**20),
    )(*results)
    return (
        grad_inputs.reshape(inputs.shape),
        grad_keys.reshape(keys.shape),
        grad_values.reshape(values.shape),
        grad_gain,
    )


def solution(mesh):
    in_specs = (
        P("pipe", "dp", "tensor", None),
        P("pipe", "dp", "tensor", None),
        P("pipe", "dp", None, "tensor"),
        P("pipe", "dp", None, "tensor"),
        P("pipe", None),
    )
    out_specs = (
        P("pipe", "dp", "tensor", None),
        P("pipe", "dp", None, "tensor"),
        P("pipe", "dp", None, "tensor"),
        P("pipe", "tensor"),
    )
    step = functools.partial(body, mesh.shape["pipe"], mesh.shape["tensor"])
    return jax.shard_map(step, mesh=mesh, in_specs=in_specs, out_specs=out_specs, check_vma=False)
```

```python
import functools
import math

import jax
import jax.numpy as jnp
from jax import lax
from jax.experimental import pallas as pl
from jax.experimental.pallas import tpu as pltpu
from jax.sharding import PartitionSpec as P

MESH = pl.DeviceIdType.MESH
HEAD_DIM = 128
EPSILON = 1e-05
ROWS = 256
FIRST = 5
AHEAD = 3
PIECES = 4
F32 = jnp.float32
BF16 = jnp.bfloat16

NT = (((1,), (1,)), ((), ()))
NN = (((1,), (0,)), ((), ()))


def dot(a, b, dims):
    return lax.dot_general(a, b, dims, preferred_element_type=F32)


def fold(x, op):
    return op(x.reshape(x.shape[0] // 8, 8, x.shape[1]), axis=0)


def kernel(
    n_pipe, n_t, heads,
    up_hbm, x_hbm, k_hbm, v_hbm, gain_hbm,
    part_ref, x_s, shift_ref, dk_ref, dv_ref, gg_ref,
    gain_s, inv_s, inv_row, inv_rows, inv_all, xh, up, go, dqs, dqr, k_s, v_s, qn_s, q_s, kt_s,
    s_s, d_s, dk_acc, dv_acc, acc_s, pg, pgr,
    x_sem, gain_sem, k_sem, v_sem, xh_send, xh_recv, up_send, up_recv,
    go_send, go_recv, dq_send, dq_recv, pg_send, pg_recv, inv_send, inv_recv, pair_sem,
):
    d = lax.axis_index("dp")
    p = lax.axis_index("pipe")
    t = lax.axis_index("tensor")
    before = lax.rem(p + n_pipe - 1, n_pipe)
    after = lax.rem(p + 1, n_pipe)
    tokens = x_s.shape[0]
    length = n_t * tokens
    width = heads * HEAD_DIM
    features = n_t * width
    mine = pl.ds(pl.multiple_of(t * tokens, tokens), tokens)

    def peer(k):
        return lax.rem(t + n_t - k, n_t)

    def columns_of(j, h):
        return pl.ds(pl.multiple_of((j * heads + h) * HEAD_DIM, HEAD_DIM), HEAD_DIM)

    barrier = pltpu.get_barrier_semaphore()

    def greet(k, carry):
        pl.semaphore_signal(barrier, inc=1, device_id=(d, p, peer(k)), device_id_type=MESH)
        return carry

    lax.fori_loop(1, n_t, greet, 0)
    second = lax.rem(t, 2)
    own_second = t - second + 1
    pl.semaphore_signal(barrier, inc=1, device_id=(d, after, own_second), device_id_type=MESH)
    pl.semaphore_signal(barrier, inc=1, device_id=(1 - d, p, own_second), device_id_type=MESH)

    load_x = pltpu.make_async_copy(x_hbm, x_s, x_sem)
    load_x.start()
    load_gain = pltpu.make_async_copy(gain_hbm, gain_s, gain_sem)
    load_gain.start()

    def head_columns(h):
        return pl.ds(pl.multiple_of(h * HEAD_DIM, HEAD_DIM), HEAD_DIM)

    def load_k(h):
        return pltpu.make_async_copy(k_hbm.at[:, head_columns(h)], k_s.at[h], k_sem.at[h])

    def load_v(h):
        return pltpu.make_async_copy(v_hbm.at[:, head_columns(h)], v_s.at[h], v_sem.at[h])

    def start_loads(h, carry):
        load_k(h).start()
        load_v(h).start()
        return carry

    load_x.wait()
    lax.fori_loop(0, heads, start_loads, 0)

    def send_input_round(h):
        def send_input(k, carry):
            to = peer(k)
            pltpu.make_async_remote_copy(
                src_ref=x_s.at[:, columns_of(to, h)], dst_ref=xh.at[h, mine, :],
                send_sem=xh_send.at[h], recv_sem=xh_recv.at[h],
                device_id=(d, p, to), device_id_type=MESH,
            ).start()
            return carry

        lax.fori_loop(1, n_t, send_input, 0)
        pltpu.make_async_copy(x_s.at[:, columns_of(t, h)], xh.at[h, mine, :], xh_recv.at[h]).start()

    def send_rows_round(h, carry):
        def send_rows(j, carry):
            pltpu.make_async_remote_copy(
                src_ref=up_hbm.at[:, columns_of(j, h)], dst_ref=up.at[h, j],
                send_sem=up_send.at[h], recv_sem=up_recv.at[h],
                device_id=(d, before, t), device_id_type=MESH,
            ).start()
            return carry

        lax.fori_loop(0, n_t, send_rows, 0)
        return carry

    @pl.when(second == 0)
    def _():
        pl.semaphore_wait(barrier, n_t - 1)
        for h in range(min(FIRST, heads)):
            send_input_round(h)
        pl.semaphore_wait(pair_sem, 1)
        lax.fori_loop(0, heads, send_rows_round, 0)

    @pl.when(second == 1)
    def _():
        pl.semaphore_wait(barrier, n_t + 3)
        pl.semaphore_signal(pair_sem, inc=1, device_id=(d, p, t - 1), device_id_type=MESH)
        send_rows_round(0, 0)
        for h in range(min(FIRST, heads)):
            send_input_round(h)
        lax.fori_loop(1, heads, send_rows_round, 0)

    def norm_rows(r, carry):
        rows = pl.ds(pl.multiple_of(r * 16, 16), 16)
        total = jnp.zeros((16, HEAD_DIM), F32)
        for c in range(n_t * heads):
            x = x_s[rows, c * HEAD_DIM : (c + 1) * HEAD_DIM].astype(F32)
            total = total + x * x
        mean = jnp.sum(total, axis=1, keepdims=True) * (1.0 / features)
        inv_s[rows, :] = jnp.broadcast_to(1.0 / jnp.sqrt(mean + EPSILON), (16, HEAD_DIM))
        return carry

    lax.fori_loop(0, tokens // 16, norm_rows, 0)
    inv_row[...] = inv_s[...].T[:8, :]

    def send_inv(k, carry):
        to = peer(k)
        pltpu.make_async_remote_copy(
            src_ref=inv_row, dst_ref=inv_rows.at[t], send_sem=inv_send, recv_sem=inv_recv,
            device_id=(d, p, to), device_id_type=MESH,
        ).start()
        return carry

    lax.fori_loop(1, n_t, send_inv, 0)
    pltpu.make_async_copy(inv_row, inv_rows.at[t], inv_recv).start()
    pg[...] = jnp.zeros_like(pg)
    load_gain.wait()

    def relay(h):
        pltpu.make_async_copy(up.at[h], up.at[h], up_recv.at[h]).wait()

        def send_grad(k, carry):
            to = peer(k)
            pltpu.make_async_remote_copy(
                src_ref=up.at[h, to], dst_ref=go.at[h, mine, :],
                send_sem=go_send.at[h], recv_sem=go_recv.at[h],
                device_id=(d, p, to), device_id_type=MESH,
            ).start()
            return carry

        lax.fori_loop(1, n_t, send_grad, 0)
        pltpu.make_async_copy(up.at[h, t], go.at[h, mine, :], go_recv.at[h]).start()

        @pl.when(h + FIRST < heads)
        def _():
            send_input_round(h + FIRST)

    to_base2 = math.log2(math.e) / math.sqrt(HEAD_DIM)
    scaling = 1.0 / math.sqrt(HEAD_DIM)
    blocks = length // ROWS
    below = lax.broadcasted_iota(jnp.int32, (ROWS, ROWS), 0) <= lax.broadcasted_iota(
        jnp.int32, (ROWS, ROWS), 1
    )

    def row_block(h, i):
        rows = pl.ds(i * ROWS, ROWS)
        q_i = q_s[rows, :]
        g_i = go[h, rows, :]
        top = None
        for c in range(i + 1):
            keys = pl.ds(c * ROWS, ROWS)
            s = dot(k_s[h, keys, :], q_i, NT)
            if c == i:
                s = jnp.where(below, s, -jnp.inf)
            s_s[keys, :] = s
            m = fold(s, jnp.max)
            top = m if top is None else jnp.maximum(top, m)
        top = jnp.max(top, axis=0, keepdims=True)
        total = jnp.zeros((8, ROWS), F32)
        weighted = jnp.zeros((8, ROWS), F32)
        for c in range(i + 1):
            keys = pl.ds(c * ROWS, ROWS)
            e = jnp.exp2((s_s[keys, :] - top) * to_base2)
            dp = dot(v_s[h, keys, :], g_i, NT)
            s_s[keys, :] = e
            d_s[keys, :] = dp
            total = total + fold(e, jnp.sum)
            weighted = weighted + fold(e * dp, jnp.sum)
        norm = 1.0 / jnp.sum(total, axis=0, keepdims=True)
        delta = jnp.sum(weighted, axis=0, keepdims=True) * norm
        norm_scaled = norm * scaling
        dq_t = jnp.zeros((HEAD_DIM, ROWS), F32)
        for c in range(i + 1):
            keys = pl.ds(c * ROWS, ROWS)
            e = s_s[keys, :]
            weights = (e * norm).astype(BF16)
            grad_s = ((e * norm_scaled) * (d_s[keys, :] - delta)).astype(BF16)
            dv = dot(weights, g_i, NN)
            dk = dot(grad_s, q_i, NN)
            if c == i:
                dv_acc[keys, :] = dv
                dk_acc[keys, :] = dk
            else:
                dv_acc[keys, :] += dv
                dk_acc[keys, :] += dk
            dq_t = dq_t + dot(kt_s[:, keys], grad_s, NN)
        dq = dq_t.T.astype(BF16)
        dqs[h, rows, :] = dq
        part = fold(dq.astype(F32) * qn_s[rows, :].astype(F32), jnp.sum)
        pg[pl.ds(h, 1), :] += jnp.sum(part, axis=0, keepdims=True)

    def send_dq_round(h):
        def send_dq(k, carry):
            to = peer(k)
            pltpu.make_async_remote_copy(
                src_ref=dqs.at[h, pl.ds(pl.multiple_of(to * tokens, tokens), tokens), :],
                dst_ref=dqr.at[h, t],
                send_sem=dq_send.at[h], recv_sem=dq_recv.at[h],
                device_id=(d, p, to), device_id_type=MESH,
            ).start()
            return carry

        lax.fori_loop(1, n_t, send_dq, 0)
        pltpu.make_async_copy(dqs.at[h, mine, :], dqr.at[h, t], dq_recv.at[h]).start()

    def head(h, carry):
        load_k(h).wait()
        load_v(h).wait()
        kt_s[...] = k_s[h].T
        pltpu.make_async_copy(xh.at[h], xh.at[h], xh_recv.at[h]).wait()
        gain_row = gain_s[pl.ds(t * heads + h, 1), :]
        normed = (xh[h].astype(F32) * inv_all[...]).astype(BF16)
        qn_s[...] = normed
        q_s[...] = (normed.astype(F32) * gain_row).astype(BF16)
        pltpu.make_async_copy(go.at[h], go.at[h], go_recv.at[h]).wait()
        for i in range(blocks):
            row_block(h, i)

        send_dq_round(h)

        @pl.when(h + AHEAD < heads)
        def _():
            relay(h + AHEAD)

        dk_ref[:, head_columns(h)] = dk_acc[...].astype(BF16)
        dv_ref[:, head_columns(h)] = dv_acc[...].astype(BF16)
        return carry

    for h in range(min(AHEAD, heads)):
        relay(h)

    pltpu.make_async_copy(inv_rows, inv_rows, inv_recv).wait()
    for j in range(n_t):
        row = jnp.broadcast_to(inv_rows[j, :1, :], (HEAD_DIM, tokens))
        inv_all[j * tokens : (j + 1) * tokens, :] = row.T
    lax.fori_loop(0, heads, head, 0)

    share = pltpu.make_async_remote_copy(
        src_ref=pg, dst_ref=pgr, send_sem=pg_send, recv_sem=pg_recv,
        device_id=(1 - d, p, t), device_id_type=MESH,
    )
    share.start()

    acc_s[...] = jnp.zeros_like(acc_s)

    def arrived(h, carry):
        pltpu.make_async_copy(dqr.at[h], dqr.at[h], dq_recv.at[h]).wait()
        acc = acc_s[...]
        inv = inv_s[...]
        for j in range(n_t):
            columns = columns_of(j, h)
            scaled = dqr[h, j].astype(F32) * gain_s[pl.ds(j * heads + h, 1), :]
            acc = acc + scaled * x_s[:, columns].astype(F32)
            part_ref[:, columns] = up[h, j].astype(F32) + scaled * inv
        acc_s[...] = acc
        return carry

    lax.fori_loop(0, heads, arrived, 0)
    inv = inv_s[...]
    shift_ref[...] = jnp.sum(acc_s[...], axis=1, keepdims=True) * (1.0 / features) * (inv * inv * inv)

    share.wait()
    summed = pg[...] + pgr[...]
    for h in range(heads):
        gg_ref[:, h * HEAD_DIM : (h + 1) * HEAD_DIM] = summed[h : h + 1, :]

    def drain(h, carry):
        many = up.at[h, pl.ds(0, n_t - 1)]
        pltpu.make_async_copy(many, many, xh_send.at[h]).wait()
        pltpu.make_async_copy(up.at[h], up.at[h], up_send.at[h]).wait()
        pltpu.make_async_copy(many, many, go_send.at[h]).wait()
        pltpu.make_async_copy(many, many, dq_send.at[h]).wait()
        return carry

    lax.fori_loop(0, heads, drain, 0)
    all_inv = inv_rows.at[pl.ds(0, n_t - 1)]
    pltpu.make_async_copy(all_inv, all_inv, inv_send).wait()


def finish_kernel(
    part_ref, x_ref, shift_ref, dk_ref, dv_ref, gg_ref,
    gi_out, dk_out, dv_out, gg_out, gi_b, sem, gi_sem,
):
    stores = [
        pltpu.make_async_copy(dk_ref, dk_out, sem.at[0]),
        pltpu.make_async_copy(dv_ref, dv_out, sem.at[1]),
        pltpu.make_async_copy(gg_ref, gg_out, sem.at[2]),
    ]
    for store in stores:
        store.start()
    width = gi_b.shape[1] // PIECES
    for j in range(PIECES):
        for c in range(j * width, (j + 1) * width, HEAD_DIM):
            columns = slice(c, c + HEAD_DIM)
            out = part_ref[:, columns] - x_ref[:, columns].astype(F32) * shift_ref[...]
            gi_b[:, columns] = out.astype(BF16)
        columns = slice(j * width, (j + 1) * width)
        store = pltpu.make_async_copy(gi_b.at[:, columns], gi_out.at[:, columns], gi_sem.at[j])
        store.start()
        stores.append(store)
    for store in stores:
        store.wait()


def body(n_pipe, n_t, upstream, inputs, keys, values, gain):
    tokens, features = inputs.shape[2:]
    length, width = keys.shape[2:]
    heads = width // HEAD_DIM
    dma = pltpu.SemaphoreType.DMA
    rounds = pltpu.VMEM((heads, n_t, tokens, HEAD_DIM), BF16)
    by_head = pltpu.VMEM((heads, length, HEAD_DIM), BF16)
    anywhere = pl.BlockSpec(memory_space=pl.ANY)
    in_vmem = pl.BlockSpec(memory_space=pltpu.VMEM)
    results = pl.pallas_call(
        functools.partial(kernel, n_pipe, n_t, heads),
        out_shape=(
            pltpu.VMEM((tokens, features), F32),
            pltpu.VMEM((tokens, features), BF16),
            pltpu.VMEM((tokens, HEAD_DIM), F32),
            pltpu.VMEM((length, width), BF16),
            pltpu.VMEM((length, width), BF16),
            pltpu.VMEM((1, width), F32),
        ),
        in_specs=[anywhere] * 5,
        out_specs=(in_vmem,) * 6,
        scratch_shapes=[
            pltpu.VMEM((n_t * heads, HEAD_DIM), F32),
            pltpu.VMEM((tokens, HEAD_DIM), F32),
            pltpu.VMEM((8, tokens), F32),
            pltpu.VMEM((n_t, 8, tokens), F32),
            pltpu.VMEM((length, HEAD_DIM), F32),
            by_head, rounds, by_head, by_head, rounds,
            by_head, by_head,
            pltpu.VMEM((length, HEAD_DIM), BF16),
            pltpu.VMEM((length, HEAD_DIM), BF16),
            pltpu.VMEM((HEAD_DIM, length), BF16),
            pltpu.VMEM((length, ROWS), F32),
            pltpu.VMEM((length, ROWS), F32),
            pltpu.VMEM((length, HEAD_DIM), F32),
            pltpu.VMEM((length, HEAD_DIM), F32),
            pltpu.VMEM((tokens, HEAD_DIM), F32),
            pltpu.VMEM((8, HEAD_DIM), F32),
            pltpu.VMEM((8, HEAD_DIM), F32),
            dma, dma,
            dma((heads,)), dma((heads,)),
            dma((heads,)), dma((heads,)), dma((heads,)), dma((heads,)),
            dma((heads,)), dma((heads,)), dma((heads,)), dma((heads,)),
            dma, dma, dma, dma,
            pltpu.SemaphoreType.REGULAR,
        ],
        compiler_params=pltpu.CompilerParams(
            collective_id=0, has_side_effects=True, vmem_limit_bytes=48 * 2**20
        ),
    )(
        upstream.reshape(tokens, features),
        inputs.reshape(tokens, features),
        keys.reshape(length, width),
        values.reshape(length, width),
        gain.reshape(n_t * heads, HEAD_DIM),
    )
    results = [pltpu.with_memory_space_constraint(r, pltpu.VMEM) for r in results]
    grad_inputs, grad_keys, grad_values, grad_gain = pl.pallas_call(
        finish_kernel,
        out_shape=(
            jax.ShapeDtypeStruct((tokens, features), BF16),
            jax.ShapeDtypeStruct((length, width), BF16),
            jax.ShapeDtypeStruct((length, width), BF16),
            jax.ShapeDtypeStruct((1, width), F32),
        ),
        in_specs=[in_vmem] * 6,
        out_specs=(anywhere,) * 4,
        scratch_shapes=[pltpu.VMEM((tokens, features), BF16), dma((3,)), dma((PIECES,))],
        compiler_params=pltpu.CompilerParams(vmem_limit_bytes=8 * 2**20),
    )(*results)
    return (
        grad_inputs.reshape(inputs.shape),
        grad_keys.reshape(keys.shape),
        grad_values.reshape(values.shape),
        grad_gain,
    )


def solution(mesh):
    in_specs = (
        P("pipe", "dp", "tensor", None),
        P("pipe", "dp", "tensor", None),
        P("pipe", "dp", None, "tensor"),
        P("pipe", "dp", None, "tensor"),
        P("pipe", None),
    )
    out_specs = (
        P("pipe", "dp", "tensor", None),
        P("pipe", "dp", None, "tensor"),
        P("pipe", "dp", None, "tensor"),
        P("pipe", "tensor"),
    )
    step = functools.partial(body, mesh.shape["pipe"], mesh.shape["tensor"])
    return jax.shard_map(step, mesh=mesh, in_specs=in_specs, out_specs=out_specs, check_vma=False)
```

```python
import functools
import math

import jax
import jax.numpy as jnp
from jax import lax
from jax.experimental import pallas as pl
from jax.experimental.pallas import tpu as pltpu
from jax.sharding import PartitionSpec as P

MESH = pl.DeviceIdType.MESH
HEAD_DIM = 128
EPSILON = 1e-05
ROWS = 256
FIRST = 5
AHEAD = 3
PIECES = 4
F32 = jnp.float32
BF16 = jnp.bfloat16

NT = (((1,), (1,)), ((), ()))
NN = (((1,), (0,)), ((), ()))


def dot(a, b, dims):
    return lax.dot_general(a, b, dims, preferred_element_type=F32)


def fold(x, op):
    return op(x.reshape(x.shape[0] // 8, 8, x.shape[1]), axis=0)


def kernel(
    n_pipe, n_t, heads,
    up_hbm, x_hbm, k_hbm, v_hbm, gain_hbm,
    part_ref, x_s, shift_ref, dk_ref, dv_ref, gg_ref,
    gain_s, inv_s, inv_row, inv_rows, inv_all, xh, up, go, dqs, dqr, k_s, v_s, qn_s, q_s, kt_s,
    s_s, d_s, dk_acc, dv_acc, acc_s, pg, pgr,
    x_sem, gain_sem, k_sem, v_sem, xh_send, xh_recv, up_send, up_recv,
    go_send, go_recv, dq_send, dq_recv, pg_send, pg_recv, inv_send, inv_recv, pair_sem,
):
    d = lax.axis_index("dp")
    p = lax.axis_index("pipe")
    t = lax.axis_index("tensor")
    before = lax.rem(p + n_pipe - 1, n_pipe)
    after = lax.rem(p + 1, n_pipe)
    tokens = x_s.shape[0]
    length = n_t * tokens
    width = heads * HEAD_DIM
    features = n_t * width
    mine = pl.ds(pl.multiple_of(t * tokens, tokens), tokens)

    def peer(k):
        return lax.rem(t + n_t - k, n_t)

    def columns_of(j, h):
        return pl.ds(pl.multiple_of((j * heads + h) * HEAD_DIM, HEAD_DIM), HEAD_DIM)

    barrier = pltpu.get_barrier_semaphore()

    def greet(k, carry):
        pl.semaphore_signal(barrier, inc=1, device_id=(d, p, peer(k)), device_id_type=MESH)
        return carry

    lax.fori_loop(1, n_t, greet, 0)
    second = lax.rem(t, 2)
    own_second = t - second + 1
    pl.semaphore_signal(barrier, inc=1, device_id=(d, after, own_second), device_id_type=MESH)
    pl.semaphore_signal(barrier, inc=1, device_id=(1 - d, p, own_second), device_id_type=MESH)

    load_x = pltpu.make_async_copy(x_hbm, x_s, x_sem)
    load_x.start()
    load_gain = pltpu.make_async_copy(gain_hbm, gain_s, gain_sem)
    load_gain.start()

    def head_columns(h):
        return pl.ds(pl.multiple_of(h * HEAD_DIM, HEAD_DIM), HEAD_DIM)

    def load_k(h):
        return pltpu.make_async_copy(k_hbm.at[:, head_columns(h)], k_s.at[h], k_sem.at[h])

    def load_v(h):
        return pltpu.make_async_copy(v_hbm.at[:, head_columns(h)], v_s.at[h], v_sem.at[h])

    def start_loads(h, carry):
        load_k(h).start()
        load_v(h).start()
        return carry

    load_x.wait()
    lax.fori_loop(0, heads, start_loads, 0)

    def send_input_round(h):
        def send_input(k, carry):
            to = peer(k)
            pltpu.make_async_remote_copy(
                src_ref=x_s.at[:, columns_of(to, h)], dst_ref=xh.at[h, mine, :],
                send_sem=xh_send.at[h], recv_sem=xh_recv.at[h],
                device_id=(d, p, to), device_id_type=MESH,
            ).start()
            return carry

        lax.fori_loop(1, n_t, send_input, 0)
        pltpu.make_async_copy(x_s.at[:, columns_of(t, h)], xh.at[h, mine, :], xh_recv.at[h]).start()

    def send_rows_round(h, carry):
        def send_rows(j, carry):
            pltpu.make_async_remote_copy(
                src_ref=up_hbm.at[:, columns_of(j, h)], dst_ref=up.at[h, j],
                send_sem=up_send.at[h], recv_sem=up_recv.at[h],
                device_id=(d, before, t), device_id_type=MESH,
            ).start()
            return carry

        lax.fori_loop(0, n_t, send_rows, 0)
        return carry

    @pl.when(second == 0)
    def _():
        pl.semaphore_wait(barrier, n_t - 1)
        for h in range(min(FIRST, heads)):
            send_input_round(h)
        pl.semaphore_wait(pair_sem, 1)
        lax.fori_loop(0, heads, send_rows_round, 0)

    @pl.when(second == 1)
    def _():
        pl.semaphore_wait(barrier, n_t + 3)
        pl.semaphore_signal(pair_sem, inc=1, device_id=(d, p, t - 1), device_id_type=MESH)
        send_rows_round(0, 0)
        for h in range(min(FIRST, heads)):
            send_input_round(h)
        lax.fori_loop(1, heads, send_rows_round, 0)

    def norm_rows(r, carry):
        rows = pl.ds(pl.multiple_of(r * 16, 16), 16)
        total = jnp.zeros((16, HEAD_DIM), F32)
        for c in range(n_t * heads):
            x = x_s[rows, c * HEAD_DIM : (c + 1) * HEAD_DIM].astype(F32)
            total = total + x * x
        mean = jnp.sum(total, axis=1, keepdims=True) * (1.0 / features)
        inv_s[rows, :] = jnp.broadcast_to(1.0 / jnp.sqrt(mean + EPSILON), (16, HEAD_DIM))
        return carry

    lax.fori_loop(0, tokens // 16, norm_rows, 0)
    inv_row[...] = inv_s[...].T[:8, :]

    def send_inv(k, carry):
        to = peer(k)
        pltpu.make_async_remote_copy(
            src_ref=inv_row, dst_ref=inv_rows.at[t], send_sem=inv_send, recv_sem=inv_recv,
            device_id=(d, p, to), device_id_type=MESH,
        ).start()
        return carry

    lax.fori_loop(1, n_t, send_inv, 0)
    pltpu.make_async_copy(inv_row, inv_rows.at[t], inv_recv).start()
    pg[...] = jnp.zeros_like(pg)
    load_gain.wait()

    def relay(h):
        pltpu.make_async_copy(up.at[h], up.at[h], up_recv.at[h]).wait()

        def send_grad(k, carry):
            to = peer(k)
            pltpu.make_async_remote_copy(
                src_ref=up.at[h, to], dst_ref=go.at[h, mine, :],
                send_sem=go_send.at[h], recv_sem=go_recv.at[h],
                device_id=(d, p, to), device_id_type=MESH,
            ).start()
            return carry

        lax.fori_loop(1, n_t, send_grad, 0)
        pltpu.make_async_copy(up.at[h, t], go.at[h, mine, :], go_recv.at[h]).start()

        @pl.when(h + FIRST < heads)
        def _():
            send_input_round(h + FIRST)

    to_base2 = math.log2(math.e) / math.sqrt(HEAD_DIM)
    scaling = 1.0 / math.sqrt(HEAD_DIM)
    blocks = length // ROWS
    below = lax.broadcasted_iota(jnp.int32, (ROWS, ROWS), 0) <= lax.broadcasted_iota(
        jnp.int32, (ROWS, ROWS), 1
    )

    def scores_of(h, i):
        s_i = s_s.at[i % 2]
        q_i = q_s[pl.ds(i * ROWS, ROWS), :]
        top = None
        for c in range(i + 1):
            keys = pl.ds(c * ROWS, ROWS)
            s = dot(k_s[h, keys, :], q_i, NT)
            if c == i:
                s = jnp.where(below, s, -jnp.inf)
            s_i[keys, :] = s
            m = fold(s, jnp.max)
            top = m if top is None else jnp.maximum(top, m)
        return jnp.max(top, axis=0, keepdims=True)

    def weights_of(h, i, top):
        s_i, d_i = s_s.at[i % 2], d_s.at[i % 2]
        g_i = go[h, pl.ds(i * ROWS, ROWS), :]
        total = jnp.zeros((8, ROWS), F32)
        weighted = jnp.zeros((8, ROWS), F32)
        for c in range(i + 1):
            keys = pl.ds(c * ROWS, ROWS)
            e = jnp.exp2((s_i[keys, :] - top) * to_base2)
            dp = dot(v_s[h, keys, :], g_i, NT)
            s_i[keys, :] = e
            d_i[keys, :] = dp
            total = total + fold(e, jnp.sum)
            weighted = weighted + fold(e * dp, jnp.sum)
        norm = 1.0 / jnp.sum(total, axis=0, keepdims=True)
        return norm, jnp.sum(weighted, axis=0, keepdims=True) * norm

    def grads_of(h, i, norm, delta):
        rows = pl.ds(i * ROWS, ROWS)
        s_i, d_i = s_s.at[i % 2], d_s.at[i % 2]
        q_i = q_s[rows, :]
        g_i = go[h, rows, :]
        norm_scaled = norm * scaling
        dq_t = jnp.zeros((HEAD_DIM, ROWS), F32)
        for c in range(i + 1):
            keys = pl.ds(c * ROWS, ROWS)
            e = s_i[keys, :]
            weights = (e * norm).astype(BF16)
            grad_s = ((e * norm_scaled) * (d_i[keys, :] - delta)).astype(BF16)
            dv = dot(weights, g_i, NN)
            dk = dot(grad_s, q_i, NN)
            if c == i:
                dv_acc[keys, :] = dv
                dk_acc[keys, :] = dk
            else:
                dv_acc[keys, :] += dv
                dk_acc[keys, :] += dk
            dq_t = dq_t + dot(kt_s[:, keys], grad_s, NN)
        dq = dq_t.T.astype(BF16)
        dqs[h, rows, :] = dq
        part = fold(dq.astype(F32) * qn_s[rows, :].astype(F32), jnp.sum)
        pg[pl.ds(h, 1), :] += jnp.sum(part, axis=0, keepdims=True)

    def send_dq_round(h):
        def send_dq(k, carry):
            to = peer(k)
            pltpu.make_async_remote_copy(
                src_ref=dqs.at[h, pl.ds(pl.multiple_of(to * tokens, tokens), tokens), :],
                dst_ref=dqr.at[h, t],
                send_sem=dq_send.at[h], recv_sem=dq_recv.at[h],
                device_id=(d, p, to), device_id_type=MESH,
            ).start()
            return carry

        lax.fori_loop(1, n_t, send_dq, 0)
        pltpu.make_async_copy(dqs.at[h, mine, :], dqr.at[h, t], dq_recv.at[h]).start()

    def head(h, carry):
        load_k(h).wait()
        load_v(h).wait()
        kt_s[...] = k_s[h].T
        pltpu.make_async_copy(xh.at[h], xh.at[h], xh_recv.at[h]).wait()
        gain_row = gain_s[pl.ds(t * heads + h, 1), :]
        normed = (xh[h].astype(F32) * inv_all[...]).astype(BF16)
        qn_s[...] = normed
        q_s[...] = (normed.astype(F32) * gain_row).astype(BF16)
        pltpu.make_async_copy(go.at[h], go.at[h], go_recv.at[h]).wait()
        ready = weights_of(h, 0, scores_of(h, 0))
        for i in range(blocks):
            after_i = weights_of(h, i + 1, scores_of(h, i + 1)) if i + 1 < blocks else None
            grads_of(h, i, *ready)
            ready = after_i

        send_dq_round(h)

        @pl.when(h + AHEAD < heads)
        def _():
            relay(h + AHEAD)

        dk_ref[:, head_columns(h)] = dk_acc[...].astype(BF16)
        dv_ref[:, head_columns(h)] = dv_acc[...].astype(BF16)
        return carry

    for h in range(min(AHEAD, heads)):
        relay(h)

    pltpu.make_async_copy(inv_rows, inv_rows, inv_recv).wait()
    for j in range(n_t):
        row = jnp.broadcast_to(inv_rows[j, :1, :], (HEAD_DIM, tokens))
        inv_all[j * tokens : (j + 1) * tokens, :] = row.T
    lax.fori_loop(0, heads, head, 0)

    share = pltpu.make_async_remote_copy(
        src_ref=pg, dst_ref=pgr, send_sem=pg_send, recv_sem=pg_recv,
        device_id=(1 - d, p, t), device_id_type=MESH,
    )
    share.start()

    acc_s[...] = jnp.zeros_like(acc_s)

    def arrived(h, carry):
        pltpu.make_async_copy(dqr.at[h], dqr.at[h], dq_recv.at[h]).wait()
        acc = acc_s[...]
        inv = inv_s[...]
        for j in range(n_t):
            columns = columns_of(j, h)
            scaled = dqr[h, j].astype(F32) * gain_s[pl.ds(j * heads + h, 1), :]
            acc = acc + scaled * x_s[:, columns].astype(F32)
            part_ref[:, columns] = up[h, j].astype(F32) + scaled * inv
        acc_s[...] = acc
        return carry

    lax.fori_loop(0, heads, arrived, 0)
    inv = inv_s[...]
    shift_ref[...] = jnp.sum(acc_s[...], axis=1, keepdims=True) * (1.0 / features) * (inv * inv * inv)

    share.wait()
    summed = pg[...] + pgr[...]
    for h in range(heads):
        gg_ref[:, h * HEAD_DIM : (h + 1) * HEAD_DIM] = summed[h : h + 1, :]

    def drain(h, carry):
        many = up.at[h, pl.ds(0, n_t - 1)]
        pltpu.make_async_copy(many, many, xh_send.at[h]).wait()
        pltpu.make_async_copy(up.at[h], up.at[h], up_send.at[h]).wait()
        pltpu.make_async_copy(many, many, go_send.at[h]).wait()
        pltpu.make_async_copy(many, many, dq_send.at[h]).wait()
        return carry

    lax.fori_loop(0, heads, drain, 0)
    all_inv = inv_rows.at[pl.ds(0, n_t - 1)]
    pltpu.make_async_copy(all_inv, all_inv, inv_send).wait()


def finish_kernel(
    part_ref, x_ref, shift_ref, dk_ref, dv_ref, gg_ref,
    gi_out, dk_out, dv_out, gg_out, gi_b, sem, gi_sem,
):
    stores = [
        pltpu.make_async_copy(dk_ref, dk_out, sem.at[0]),
        pltpu.make_async_copy(dv_ref, dv_out, sem.at[1]),
        pltpu.make_async_copy(gg_ref, gg_out, sem.at[2]),
    ]
    for store in stores:
        store.start()
    width = gi_b.shape[1] // PIECES
    for j in range(PIECES):
        for c in range(j * width, (j + 1) * width, HEAD_DIM):
            columns = slice(c, c + HEAD_DIM)
            out = part_ref[:, columns] - x_ref[:, columns].astype(F32) * shift_ref[...]
            gi_b[:, columns] = out.astype(BF16)
        columns = slice(j * width, (j + 1) * width)
        store = pltpu.make_async_copy(gi_b.at[:, columns], gi_out.at[:, columns], gi_sem.at[j])
        store.start()
        stores.append(store)
    for store in stores:
        store.wait()


def body(n_pipe, n_t, upstream, inputs, keys, values, gain):
    tokens, features = inputs.shape[2:]
    length, width = keys.shape[2:]
    heads = width // HEAD_DIM
    dma = pltpu.SemaphoreType.DMA
    rounds = pltpu.VMEM((heads, n_t, tokens, HEAD_DIM), BF16)
    by_head = pltpu.VMEM((heads, length, HEAD_DIM), BF16)
    anywhere = pl.BlockSpec(memory_space=pl.ANY)
    in_vmem = pl.BlockSpec(memory_space=pltpu.VMEM)
    results = pl.pallas_call(
        functools.partial(kernel, n_pipe, n_t, heads),
        out_shape=(
            pltpu.VMEM((tokens, features), F32),
            pltpu.VMEM((tokens, features), BF16),
            pltpu.VMEM((tokens, HEAD_DIM), F32),
            pltpu.VMEM((length, width), BF16),
            pltpu.VMEM((length, width), BF16),
            pltpu.VMEM((1, width), F32),
        ),
        in_specs=[anywhere] * 5,
        out_specs=(in_vmem,) * 6,
        scratch_shapes=[
            pltpu.VMEM((n_t * heads, HEAD_DIM), F32),
            pltpu.VMEM((tokens, HEAD_DIM), F32),
            pltpu.VMEM((8, tokens), F32),
            pltpu.VMEM((n_t, 8, tokens), F32),
            pltpu.VMEM((length, HEAD_DIM), F32),
            by_head, rounds, by_head, by_head, rounds,
            by_head, by_head,
            pltpu.VMEM((length, HEAD_DIM), BF16),
            pltpu.VMEM((length, HEAD_DIM), BF16),
            pltpu.VMEM((HEAD_DIM, length), BF16),
            pltpu.VMEM((2, length, ROWS), F32),
            pltpu.VMEM((2, length, ROWS), F32),
            pltpu.VMEM((length, HEAD_DIM), F32),
            pltpu.VMEM((length, HEAD_DIM), F32),
            pltpu.VMEM((tokens, HEAD_DIM), F32),
            pltpu.VMEM((8, HEAD_DIM), F32),
            pltpu.VMEM((8, HEAD_DIM), F32),
            dma, dma,
            dma((heads,)), dma((heads,)),
            dma((heads,)), dma((heads,)), dma((heads,)), dma((heads,)),
            dma((heads,)), dma((heads,)), dma((heads,)), dma((heads,)),
            dma, dma, dma, dma,
            pltpu.SemaphoreType.REGULAR,
        ],
        compiler_params=pltpu.CompilerParams(
            collective_id=0, has_side_effects=True, vmem_limit_bytes=48 * 2**20
        ),
    )(
        upstream.reshape(tokens, features),
        inputs.reshape(tokens, features),
        keys.reshape(length, width),
        values.reshape(length, width),
        gain.reshape(n_t * heads, HEAD_DIM),
    )
    results = [pltpu.with_memory_space_constraint(r, pltpu.VMEM) for r in results]
    grad_inputs, grad_keys, grad_values, grad_gain = pl.pallas_call(
        finish_kernel,
        out_shape=(
            jax.ShapeDtypeStruct((tokens, features), BF16),
            jax.ShapeDtypeStruct((length, width), BF16),
            jax.ShapeDtypeStruct((length, width), BF16),
            jax.ShapeDtypeStruct((1, width), F32),
        ),
        in_specs=[in_vmem] * 6,
        out_specs=(anywhere,) * 4,
        scratch_shapes=[pltpu.VMEM((tokens, features), BF16), dma((3,)), dma((PIECES,))],
        compiler_params=pltpu.CompilerParams(vmem_limit_bytes=8 * 2**20),
    )(*results)
    return (
        grad_inputs.reshape(inputs.shape),
        grad_keys.reshape(keys.shape),
        grad_values.reshape(values.shape),
        grad_gain,
    )


def solution(mesh):
    in_specs = (
        P("pipe", "dp", "tensor", None),
        P("pipe", "dp", "tensor", None),
        P("pipe", "dp", None, "tensor"),
        P("pipe", "dp", None, "tensor"),
        P("pipe", None),
    )
    out_specs = (
        P("pipe", "dp", "tensor", None),
        P("pipe", "dp", None, "tensor"),
        P("pipe", "dp", None, "tensor"),
        P("pipe", "tensor"),
    )
    step = functools.partial(body, mesh.shape["pipe"], mesh.shape["tensor"])
    return jax.shard_map(step, mesh=mesh, in_specs=in_specs, out_specs=out_specs, check_vma=False)
```
